128 devices in a mesh: tm: 8 (over x_lo, z), height: 16 (over y, x_hi, core).
Axes of the slice: x: 4 (x_hi: 2, x_lo: 2; x = x_hi * 2 + x_lo), y: 4, z: 4, core: 2. Of those that a mesh axis runs over, the one named last changes fastest.
Arguments:
- queries: bfloat16 [32, 32, 16, 2560], P('tm', 'height'), may hold values from -64 to 64
- keys: bfloat16 [32, 32, 16, 2560], P('tm', 'height'), may hold values from -64 to 64
- values: bfloat16 [32, 32, 16, 2560], P('tm', 'height'), may hold values from -6 to 6
- tile_mask: int32 [8, 16, 2, 18], P('tm', 'height'), may hold values 0 or 1
- sink_frame: int32 [1], replicated, may hold values from 0 to 31
Outputs:
- attended: bfloat16 [32, 32, 16, 2560], P('tm', 'height')
The draws below stay inside these ranges and needn't reach their ends.
All inputs are finite; a program needn't handle non-finite values. No bound on the sum of `tile_mask` on one device may be relied on, other than what follows from the above.
Results may differ from the reference program's by a relative error of at most 0.0041.
Values may be sent and summed in bfloat16 or wider, within the bound.
A program may use at most 128 MiB of HBM per device.

```python
import math
import jax
import jax.numpy as jnp
from jax import lax

H = 20
HD = 128
TF = 4
TR = 2
TC = 8
COLS = 16
NEIGHBOURS = 18
FRAMES = 32
BANDS = 16
ROWS = 32
E = 2560
TT = 8
TW = 2


def shared_fields(key):
    shape = (FRAMES * ROWS * COLS, H * HD)
    key_field = jnp.clip(jax.random.normal(jax.random.fold_in(key, 21), shape, jnp.float32), -4.0, 4.0)
    query_field = jnp.clip(jax.random.normal(jax.random.fold_in(key, 22), shape, jnp.float32), -4.0, 4.0)
    final_shape = (FRAMES, ROWS, COLS, H * HD)
    return (query_field.reshape(final_shape), key_field.reshape(final_shape))


def draw_queries(key, part):
    return shared_fields(key)[0].astype(jnp.bfloat16)


def draw_keys(key, part):
    return shared_fields(key)[1].astype(jnp.bfloat16)


def with_ends(entries, rng, least, high):
    extent = entries.shape
    index_at = [jax.random.randint(jax.random.fold_in(rng, axis), (), 0, extent[axis]) for axis in range(len(extent))]
    entries = entries.at[tuple(index_at)].set(least)
    longest = extent.index(max(extent))
    index_at[longest] = (index_at[longest] + 1) % extent[longest]
    return entries.at[tuple(index_at)].set(high)


def shard_levels(stream_key, dims, cuts, low, high):
    def one(dim, shards_of):
        draws = jax.random.uniform(jax.random.fold_in(jax.random.fold_in(stream_key, 6), dim), (shards_of,), jnp.float32, low / len(cuts), high / len(cuts))
        return jnp.repeat(jnp.exp(draws), dims[dim] // shards_of).reshape((-1,) + (1,) * (len(dims) - dim - 1))

    factor_of = one(*cuts[0])
    for cut in cuts[1:]:
        factor_of = factor_of * one(*cut)
    return factor_of


def scatter_about(key, dims, width, bound, split=(), kind=jnp.bfloat16):
    drawn = jax.random.normal(key, dims, jnp.float32) * width
    if len(split) > 0:
        drawn = shard_levels(key, dims, split, -0.22, 0.18) * drawn
    return jnp.clip(drawn, min=-bound, max=bound).astype(kind)


def setup_inputs(seed: int = 0) -> dict:
    key_of = jax.random.split(jax.random.key(seed), 6)
    queries = draw_queries(jax.random.fold_in(key_of[5], 71), 0)
    keys = draw_keys(jax.random.fold_in(key_of[5], 71), 0)
    values = scatter_about(key_of[2], (FRAMES, ROWS, COLS, E), 1.0, 6.0, ((0, 8), (1, 16)))
    tile_mask = with_ends((jax.random.randint(key_of[3], (TT, BANDS, TW, NEIGHBOURS), 0, 4) < 3).astype(jnp.int32), jax.random.fold_in(key_of[3], 1), 0, 1)
    sink_frame = jax.random.randint(key_of[4], (1,), 0, FRAMES).astype(jnp.int32)
    return dict(queries=queries, keys=keys, values=values, tile_mask=tile_mask, sink_frame=sink_frame)


masked_score = -1e+30

def tile_allowed(tile_flags, time_base, band_index, band_total):
    q_tiles = tile_flags.shape[0]
    w_tiles = tile_flags.shape[1]
    q_time = jnp.arange(q_tiles)[:, None, None, None, None]
    q_width = jnp.arange(w_tiles)[None, :, None, None, None]
    k_time = jnp.arange(q_tiles + 1)[None, None, :, None, None]
    k_band = jnp.arange(3)[None, None, None, :, None] - 1
    k_width = jnp.arange(w_tiles)[None, None, None, None, :]
    time_step = k_time - 1 - q_time
    width_step = k_width - q_width
    nearby = (time_step >= -1) & (time_step <= 0) & (jnp.abs(width_step) <= 1)
    code_all = (time_step + 1) * 9 + (k_band + 1) * 3 + width_step + 1
    matches = code_all[..., None] == jnp.arange(tile_flags.shape[2])
    picked = lax.optimization_barrier(jnp.sum(jnp.where(matches, tile_flags[:, :, None, None, None, :], 0), axis=-1)) > 0
    itself = (time_step == 0) & (k_band == 0) & (width_step == 0)
    time_valid = time_base + k_time - 1 >= 0
    band_now = band_index + k_band
    band_valid = (band_now >= 0) & (band_now < band_total)
    return nearby & (picked | itself) & time_valid & band_valid

def token_allowed(tiles_ok, row_count):
    q_tiles, w_tiles, k_tiles = (tiles_ok.shape[0], tiles_ok.shape[1], tiles_ok.shape[2])
    grid = tiles_ok[:, None, None, :, None, :, None, :, None, :, None]
    full = jnp.broadcast_to(grid, (q_tiles, TF, row_count, w_tiles, TC, k_tiles, TF, 3, row_count, w_tiles, TC))
    return full.reshape(q_tiles * TF * row_count * w_tiles * TC, k_tiles * TF * 3 * row_count * w_tiles * TC)

def reference(queries, keys, values, tile_mask, sink_frame):
    scaling = 1.0 / math.sqrt(HD)
    key_pad = jnp.pad(keys, ((TF, 0), (TR, TR), (0, 0), (0, 0)))
    val_pad = jnp.pad(values, ((TF, 0), (TR, TR), (0, 0), (0, 0)))
    sink_index = sink_frame[0].astype(jnp.int32)
    sink_keys = lax.dynamic_index_in_dim(keys, sink_index, 0, keepdims=False).reshape(BANDS, TR * COLS, H, HD).astype(jnp.float32)
    sink_vals = lax.dynamic_index_in_dim(values, sink_index, 0, keepdims=False).reshape(BANDS, TR * COLS, H, HD).astype(jnp.float32)
    zero_index = jnp.zeros((), jnp.int32)

    def one_tile(tile_index):
        time_tile = (tile_index // BANDS).astype(jnp.int32)
        band_index = (tile_index % BANDS).astype(jnp.int32)
        q_block = lax.dynamic_slice(queries, (time_tile * TF, band_index * TR, zero_index, zero_index), (TF, TR, COLS, E))
        q_block = q_block.reshape(TF * TR * COLS, H, HD).astype(jnp.float32)
        k_block = lax.dynamic_slice(key_pad, (time_tile * TF, band_index * TR, zero_index, zero_index), (2 * TF, 3 * TR, COLS, E))
        k_block = k_block.reshape(-1, H, HD).astype(jnp.float32)
        v_block = lax.dynamic_slice(val_pad, (time_tile * TF, band_index * TR, zero_index, zero_index), (2 * TF, 3 * TR, COLS, E))
        v_block = v_block.reshape(-1, H, HD).astype(jnp.float32)
        tile_flags = lax.dynamic_slice(tile_mask, (time_tile, band_index, zero_index, zero_index), (1, 1, TW, NEIGHBOURS))[:, 0]
        allowed = token_allowed(tile_allowed(tile_flags, time_tile, band_index, BANDS), TR)
        scores = jnp.einsum('qhd,khd->hqk', q_block, k_block) * scaling
        scores = jnp.where(allowed[None], scores, masked_score)
        row_max = lax.optimization_barrier(jnp.max(scores, axis=-1))
        weights = jnp.exp(scores - row_max[..., None]).astype(jnp.bfloat16).astype(jnp.float32)
        row_sum = lax.optimization_barrier(jnp.sum(weights, axis=-1))
        window_out = jnp.einsum('hqk,khd->hqd', weights, v_block)
        sink_scores = jnp.einsum('qhd,rkhd->hqrk', q_block, sink_keys) * scaling
        sink_max = lax.optimization_barrier(jnp.max(sink_scores, axis=-1))
        sink_weights = jnp.exp(sink_scores - sink_max[..., None]).astype(jnp.bfloat16).astype(jnp.float32)
        sink_sum = lax.optimization_barrier(jnp.sum(sink_weights, axis=-1))
        top_score = jnp.maximum(row_max, lax.optimization_barrier(jnp.max(sink_max, axis=-1)))
        window_factor = jnp.exp(row_max - top_score)
        sink_factor = jnp.exp(sink_max - top_score[..., None])
        sink_out = jnp.einsum('hqrk,rkhd->hqd', sink_weights * sink_factor[..., None], sink_vals)
        numerator = window_factor[..., None] * window_out + sink_out
        denominator = window_factor * row_sum + lax.optimization_barrier(jnp.sum(sink_factor * sink_sum, axis=-1))
        result = numerator / denominator[..., None]
        return jnp.transpose(result, (1, 0, 2)).reshape(TF, TR, COLS, E).astype(jnp.bfloat16)
    blocks = lax.map(one_tile, jnp.arange(TT * BANDS, dtype=jnp.int32))
    blocks = blocks.reshape(TT, BANDS, TF, TR, COLS, E)
    return jnp.transpose(blocks, (0, 2, 1, 3, 4, 5)).reshape(FRAMES, ROWS, COLS, E)
```

```python
import math

import jax
import jax.numpy as jnp
from jax import lax
from jax.experimental import pallas as pl
from jax.experimental.pallas import tpu as pltpu
from jax.sharding import PartitionSpec as P

H = 20
HD = 128
TF = 4
TC = 8
COLS = 16
E = H * HD
TOK = 128
SINK = 32
HALF = E // 2
CHUNK = 2 * HD
CHUNKS = E // CHUNK
EARLY = 3
MASKED = -1e30
SCALE = math.log2(math.e) / math.sqrt(HD)
MESH = pl.DeviceIdType.MESH
F32, BF16 = jnp.float32, jnp.bfloat16


def attend(q_hbm, k_hbm, v_hbm, mask_ref, sink_ref, out_ref,
           qbuf, kbuf, vbuf, flags, bias, sel, zin, zsum, xin, skv, ones, part, back, ours, stats, theirs,
           local_sem, halo_s, halo_r, core_s, core_r, q_s, q_r, flag_s, flag_r, z_s, z_r, lo_s, lo_r,
           x_s, x_r, y_s, y_r, f_s, f_r, o_s, o_r, st_s, st_r):
    tm, h = lax.axis_index("tm"), lax.axis_index("height")
    lo, z, y, hi, c = tm // 4, tm % 4, h // 4, (h // 2) % 2, h % 2
    x = hi * 2 + lo
    parity = tm % 2

    def at(x, y, z, c):
        x, y, z = (x + 4) % 4, (y + 4) % 4, (z + 4) % 4
        return ((x % 2) * 4 + z, y * 4 + (x // 2) * 2 + c)

    partner = at(x, y, z, 1 - c)
    beyond = (tm, (h + 2 * c - 1 + 16) % 16)
    earlier, later = ((tm + 7) % 8, h), ((tm + 1) % 8, h)
    z_mates = [at(x, y, z + d, c) for d in (1, -1, 2)]
    x_mates = [at(x + d, y, z, c) for d in (1, -1, 2)]
    y_mates = [at(x, y + d, z, c) for d in (1, -1, 2)]
    lo_mate = at(hi * 2 + 1 - lo, y, z, c)

    def remote(src, dst, send, recv, device):
        return pltpu.make_async_remote_copy(src, dst, send, recv, device_id=device, device_id_type=MESH)

    local = [
        pltpu.make_async_copy(k_hbm, kbuf.at[pl.ds(TOK, TOK)], local_sem.at[0]),
        pltpu.make_async_copy(v_hbm, vbuf.at[pl.ds(TOK, TOK)], local_sem.at[1]),
        pltpu.make_async_copy(q_hbm, qbuf.at[pl.ds(0, TOK)], local_sem.at[2]),
    ]
    for copy in local:
        copy.start()
    barrier = pltpu.get_barrier_semaphore()
    friends = [partner, beyond, earlier, later, *z_mates, *x_mates, *y_mates]
    for friend in friends:
        pl.semaphore_signal(barrier, inc=1, device_id=friend, device_id_type=MESH)

    flags[0] = jnp.zeros((8, 128), F32)
    flags[0, 0:2, 0:18] = mask_ref[...].astype(F32)
    stats[...] = jnp.zeros_like(stats)
    ones[...] = jnp.ones_like(ones)
    for copy in local:
        copy.wait()

    frame = (sink_ref[0] - tm * TF).astype(F32)
    for i, buf in enumerate((kbuf, vbuf)):
        tokens = 0.0
        for f in range(TF):
            mine = jnp.where(frame == f, 1.0, 0.0).astype(F32)
            tokens = tokens + buf[TOK + f * SINK:TOK + (f + 1) * SINK, :].astype(F32) * mine
        tokens = tokens.astype(BF16)
        sel[0, i] = tokens[:, :HALF]
        sel[1, i] = tokens[:, HALF:]
    pl.semaphore_wait(barrier, len(friends))

    def place(step, par):
        half = jnp.where(step < CHUNKS // 2, 1 - par, par)
        return pl.multiple_of(half * HALF + (step % (CHUNKS // 2)) * CHUNK, CHUNK)

    def halo(step):
        lanes = pl.ds(place(step, parity), CHUNK)
        return [
            remote(buf.at[pl.ds(TOK, TOK), lanes], buf.at[pl.ds(2 * TOK, TOK), lanes],
                   halo_s.at[i, step], halo_r.at[i, step], beyond)
            for i, buf in enumerate((kbuf, vbuf))
        ]

    def q_out(step, par):
        lanes = pl.ds(place(step, par), CHUNK)
        return remote(qbuf.at[pl.ds(0, TOK), lanes], qbuf.at[pl.ds(TOK, TOK), lanes],
                      q_s.at[step], q_r.at[step], earlier)

    def send(step):
        for copy in halo(step):
            copy.start()
        q_out(step, 1 - parity).start()

    def o_back(step):
        lanes = pl.ds(place(step, parity), CHUNK)
        return remote(part.at[:, lanes], back.at[:, lanes], o_s.at[step], o_r.at[step], later)

    to_z = [
        remote(sel.at[half], zin.at[i], z_s.at[i], z_r.at[i], mate)
        for i, (half, mate) in enumerate(zip((1 - parity, 1 - parity, parity), z_mates))
    ]
    flag_copy = remote(flags.at[0], flags.at[1], flag_s, flag_r, earlier)
    core_copies = [
        remote(buf.at[pl.ds(TOK, TOK)], buf.at[pl.ds(0, TOK)], core_s.at[i], core_r.at[i], partner)
        for i, buf in enumerate((kbuf, vbuf))
    ]
    for copy in to_z:
        copy.start()
    flag_copy.start()
    for step in range(EARLY):
        send(step)
    for copy in core_copies:
        copy.start()

    def make_bias():
        lane = lax.broadcasted_iota(jnp.int32, (1, TOK), 1)
        key_first = (lane % COLS) < TC
        rows = lax.broadcasted_iota(jnp.int32, (TOK, TOK), 0)
        query_first = (rows % COLS) < TC
        at_zero = (1 - c).astype(F32)
        at_one = c.astype(F32)
        band_ok = jnp.where((h + 2 * c - 1 >= 0) & (h + 2 * c - 1 < 16), 1.0, 0.0).astype(F32)
        time_ok = jnp.where(tm < 7, 1.0, 0.0).astype(F32)
        for which, base in ((0, 9), (1, 0)):
            def flag(cq, dh, dw):
                code = base + dh * 3 + dw
                return flags[which, cq:cq + 1, code:code + 1]

            for slot in range(3):
                lines = []
                for cq in range(2):
                    pair = []
                    for ck in range(2):
                        dw = ck - cq + 1
                        if slot == 1:
                            value = flag(cq, 1, dw)
                            if which == 0 and dw == 1:
                                value = jnp.ones_like(value)
                        else:
                            first, second = (2, 0) if slot == 0 else (0, 2)
                            value = flag(cq, first, dw) * at_zero + flag(cq, second, dw) * at_one
                        if slot == 2:
                            value = value * band_ok
                        if which == 1:
                            value = value * time_ok
                        pair.append(value)
                    lines.append(jnp.where(key_first, pair[0], pair[1]))
                allowed = jnp.where(query_first, lines[0], lines[1])
                bias[which * TOK:(which + 1) * TOK, slot * TOK:(slot + 1) * TOK] = jnp.where(
                    allowed > 0.5, 0.0, MASKED
                )

    def head(lane, sink_lane, number):
        lanes = pl.ds(lane, HD)
        q = qbuf[:, lanes]
        contract = (((1,), (1,)), ((), ()))
        scores = lax.dot_general(q, kbuf[:, lanes], contract, preferred_element_type=F32) + bias[...]
        top = jnp.max(scores, axis=1, keepdims=True)
        if sink_lane is not None:
            lines = pl.ds(sink_lane, HD)
            sink_k = skv[:, :, 0, :, lines].reshape(512, HD)
            sink_v = skv[:, :, 1, :, lines].reshape(512, HD)
            sink_scores = lax.dot_general(q, sink_k, contract, preferred_element_type=F32)
            top = jnp.maximum(top, jnp.max(sink_scores, axis=1, keepdims=True))
        probs = jnp.exp2((scores - top) * SCALE).astype(BF16)
        vals = jnp.concatenate([vbuf[:, lanes], ones[0:3 * TOK]], axis=1)
        total = jnp.dot(probs, vals, preferred_element_type=F32)
        if sink_lane is not None:
            sink_probs = jnp.exp2((sink_scores - top) * SCALE).astype(BF16)
            vals = jnp.concatenate([sink_v, ones[...]], axis=1)
            total = total + jnp.dot(sink_probs, vals, preferred_element_type=F32)
        weighted, norm = total[:, :HD], total[:, HD:]
        ours[:, lanes] = weighted[:TOK]
        part[:, lanes] = (weighted[TOK:] / norm[TOK:]).astype(BF16)
        spot = lax.broadcasted_iota(jnp.int32, (2 * TOK, 128), 1)
        stats[...] = jnp.where(spot == number, top, jnp.where(spot == number + 64, norm, stats[...]))

    def chunk(step, with_sink):
        for copy in halo(step):
            copy.wait_recv()
        q_out(step, 1 - parity).wait_recv()
        lane = place(step, parity)
        for i in range(CHUNK // HD):
            sink_lane = None
            if with_sink:
                sink_lane = pl.multiple_of((step % (CHUNKS // 2)) * CHUNK + i * HD, HD)
            head(pl.multiple_of(lane + i * HD, HD), sink_lane, lane // HD + i)
        o_back(step).start()

    make_sum = [sel.at[parity], zin.at[0], zin.at[1], zin.at[2]]
    for copy in to_z:
        copy.wait_recv()
    zsum[...] = sum(ref[...].astype(F32) for ref in make_sum).astype(BF16)
    lo_copy = remote(zsum.at[1 - lo], xin, lo_s, lo_r, lo_mate)
    lo_copy.start()
    send(EARLY)
    flag_copy.wait_recv()
    make_bias()
    for copy in core_copies:
        copy.wait_recv()
    chunk(0, False)
    lo_copy.wait_recv()
    own = skv.at[0, 0, lo, pl.ds(pl.multiple_of(hi * SINK, SINK), SINK)]
    own[...] = (zsum[lo].astype(F32) + xin[...].astype(F32)).astype(BF16)
    to_x = [remote(own, own, x_s.at[i], x_r.at[i], mate) for i, mate in enumerate(x_mates)]
    for copy in to_x:
        copy.start()
    for step in range(EARLY + 1, CHUNKS):
        send(step)
    chunk(1, False)
    chunk(2, False)

    def place_of(xx):
        xx = (xx + 4) % 4
        return skv.at[0, 0, xx % 2, pl.ds(pl.multiple_of((xx // 2) * SINK, SINK), SINK)]

    for i, d in enumerate((-1, 1, 2)):
        remote(own, place_of(x + d), x_s.at[i], x_r.at[i], x_mates[i]).wait_recv()
    to_y = [remote(skv.at[0, 0], skv.at[i + 1, 0], y_s.at[i], y_r.at[i], mate) for i, mate in enumerate(y_mates)]
    across = [remote(skv.at[i, 0], skv.at[i, 1], f_s.at[i], f_r.at[i], partner) for i in range(4)]
    for copy in to_y:
        copy.start()
    across[0].start()
    chunk(3, False)
    chunk(4, False)
    for i in range(3):
        to_y[i].wait_recv()
        across[i + 1].start()
    for copy in across:
        copy.wait_recv()

    def sink_chunk(step, carry):
        chunk(step, True)
        return carry

    lax.fori_loop(CHUNKS // 2, CHUNKS, sink_chunk, 0)
    st_copy = remote(stats.at[pl.ds(TOK, TOK)], theirs, st_s, st_r, later)
    st_copy.start()
    st_copy.wait_recv()
    for step in range(CHUNKS):
        remote(part.at[:, pl.ds(0, CHUNK)], back.at[:, pl.ds(place(step, 1 - parity), CHUNK)],
               o_s.at[step], o_r.at[step], later).wait_recv()

    top_a, top_b = stats[0:TOK], theirs[...]
    norm_a, norm_b = pltpu.roll(top_a, 64, 1), pltpu.roll(top_b, 64, 1)
    top = jnp.maximum(top_a, top_b)
    weight_a = jnp.exp2((top_a - top) * SCALE)
    weight_b = jnp.exp2((top_b - top) * SCALE) * norm_b
    inverse = 1.0 / (weight_a * norm_a + weight_b)
    weight_a, weight_b = weight_a * inverse, weight_b * inverse
    for i in range(H):
        lanes = slice(i * HD, (i + 1) * HD)
        out_ref[:, lanes] = (
            weight_a[:, i:i + 1] * ours[:, lanes] + weight_b[:, i:i + 1] * back[:, lanes].astype(F32)
        ).astype(BF16)

    for copy in [*to_z, flag_copy, *core_copies, lo_copy, *to_x, *to_y, *across, st_copy]:
        copy.wait_send()
    for step in range(CHUNKS):
        for copy in halo(step):
            copy.wait_send()
        q_out(step, 1 - parity).wait_send()
        o_back(step).wait_send()


def shards(queries, keys, values, tile_mask, sink_frame):
    any_spec, vmem, smem = (pl.BlockSpec(memory_space=space) for space in (pl.ANY, pltpu.VMEM, pltpu.SMEM))
    sems = pltpu.SemaphoreType.DMA
    out = pl.pallas_call(
        attend,
        out_shape=jax.ShapeDtypeStruct((TOK, E), BF16),
        in_specs=[any_spec, any_spec, any_spec, vmem, smem],
        out_specs=vmem,
        scratch_shapes=[
            pltpu.VMEM((2 * TOK, E), BF16),
            pltpu.VMEM((3 * TOK, E), BF16),
            pltpu.VMEM((3 * TOK, E), BF16),
            pltpu.VMEM((2, 8, 128), F32),
            pltpu.VMEM((2 * TOK, 3 * TOK), F32),
            pltpu.VMEM((2, 2, SINK, HALF), BF16),
            pltpu.VMEM((3, 2, SINK, HALF), BF16),
            pltpu.VMEM((2, SINK, HALF), BF16),
            pltpu.VMEM((SINK, HALF), BF16),
            pltpu.VMEM((4, 2, 2, 2 * SINK, HALF), BF16),
            pltpu.VMEM((4 * TOK, HD), BF16),
            pltpu.VMEM((TOK, E), BF16),
            pltpu.VMEM((TOK, E), BF16),
            pltpu.VMEM((TOK, E), F32),
            pltpu.VMEM((2 * TOK, 128), F32),
            pltpu.VMEM((TOK, 128), F32),
            sems((3,)),
            sems((2, CHUNKS)), sems((2, CHUNKS)),
            sems((2,)), sems((2,)),
            sems((CHUNKS,)), sems((CHUNKS,)),
            sems, sems,
            sems((3,)), sems((3,)),
            sems, sems,
            sems((3,)), sems((3,)),
            sems((3,)), sems((3,)),
            sems((4,)), sems((4,)),
            sems((CHUNKS,)), sems((CHUNKS,)),
            sems, sems,
        ],
        compiler_params=pltpu.CompilerParams(
            collective_id=0, has_side_effects=True, vmem_limit_bytes=48 * 2**20
        ),
        cost_estimate=pl.CostEstimate(flops=2 * 10**9, bytes_accessed=3 * 10**6, transcendentals=4 * 10**6),
    )(
        queries.reshape(TOK, E), keys.reshape(TOK, E), values.reshape(TOK, E),
        tile_mask.reshape(2, 18), sink_frame,
    )
    return out.reshape(queries.shape)


def solution(mesh):
    spec = P("tm", "height", None, None)
    return jax.shard_map(
        shards,
        mesh=mesh,
        in_specs=(spec, spec, spec, spec, P()),
        out_specs=spec,
        check_vma=False,
    )
```

```python
import math

import jax
import jax.numpy as jnp
from jax import lax
from jax.experimental import pallas as pl
from jax.experimental.pallas import tpu as pltpu
from jax.sharding import PartitionSpec as P

H = 20
HD = 128
TF = 4
TC = 8
COLS = 16
E = H * HD
TOK = 128
SINK = 32
G = 5
GE = G * HD
BANDS = 4
EARLY = 2
MASKED = -1e30
SCALE = math.log2(math.e) / math.sqrt(HD)
MESH = pl.DeviceIdType.MESH
F32, BF16 = jnp.float32, jnp.bfloat16


def attend(q_hbm, k_hbm, v_hbm, mask_hbm, sink_ref, out_ref,
           mask_ref, qsrc, kvsrc, flags, flags_in, flags_next, bias, sel, xin, zown, zin, skv, ones,
           q_in, q_next, kv, part, back, stat, stat_in, ours, our_top, our_sum, outs,
           local_sem, fx_s, fx_r, fz_s, fz_r, kv_s, kv_r, q_s, q_r, y_s, y_r, n_s, n_r, b_s, b_r, st_s, st_r,
           sx_s, sx_r, sz_s, sz_r, sy_s, sy_r, sc_s, sc_r, o_s, o_r):
    tm, h = lax.axis_index("tm"), lax.axis_index("height")
    lo, z, y, hi, c = tm // 4, tm % 4, h // 4, (h // 2) % 2, h % 2
    x = hi * 2 + lo
    time = z + 4 * c

    def at(x, y, z, c):
        x, y, z = (x + 4) % 4, (y + 4) % 4, (z + 4) % 4
        return ((x % 2) * 4 + z, y * 4 + (x // 2) * 2 + c)

    def at_time(t):
        t = (t + 8) % 8
        return at(x, y, t % 4, t // 4)

    partner = at(x, y, z, 1 - c)
    earlier, later = at_time(time - 1), at_time(time + 1)
    steps = (1, -1, 2)
    y_mates = [at(x, y + d, z, c) for d in steps]
    z_mates = [at(x, y, z + d, c) for d in steps]

    def remote(src, dst, send, recv, device):
        return pltpu.make_async_remote_copy(src, dst, send, recv, device_id=device, device_id_type=MESH)

    local = [
        pltpu.make_async_copy(k_hbm, kvsrc.at[0], local_sem.at[0]),
        pltpu.make_async_copy(v_hbm, kvsrc.at[1], local_sem.at[1]),
        pltpu.make_async_copy(q_hbm, qsrc, local_sem.at[2]),
        pltpu.make_async_copy(mask_hbm, mask_ref, local_sem.at[3]),
    ]
    for copy in local:
        copy.start()
    barrier = pltpu.get_barrier_semaphore()
    friends = [at(x + d, y, z, core) for d in steps for core in range(2)]
    friends += [partner, earlier, later, *y_mates, *z_mates]
    for friend in friends:
        pl.semaphore_signal(barrier, inc=1, device_id=friend, device_id_type=MESH)
    ones[...] = jnp.ones_like(ones)
    stat[...] = jnp.zeros_like(stat)
    flags[...] = jnp.zeros_like(flags)
    for copy in local:
        copy.wait()
    flags[0:2, 0:18] = mask_ref[...].astype(F32)

    frame = (sink_ref[0] - tm * TF).astype(F32)
    for i in range(2):
        tokens = 0.0
        for f in range(TF):
            mine = jnp.where(frame == f, 1.0, 0.0).astype(F32)
            tokens = tokens + kvsrc[i, f * SINK:(f + 1) * SINK, :].astype(F32) * mine
        sel[i] = tokens.astype(BF16)
    pl.semaphore_wait(barrier, len(friends))

    def own_lanes(xx):
        return pl.ds(pl.multiple_of(((xx + 4) % 4) * GE, HD), GE)

    band = hi * 2 + c

    class Either:
        def __init__(self, src, dst, send, recv, device, here):
            self.far = lambda: remote(src, dst, send, recv, device)
            self.near = lambda: pltpu.make_async_copy(src, dst, recv)
            self.here = here

        def start(self):
            pl.when(self.here)(lambda: self.near().start())
            pl.when(jnp.logical_not(self.here))(lambda: self.far().start())

        def wait_send(self):
            pl.when(jnp.logical_not(self.here))(lambda: self.far().wait_send())

        def wait_recv(self):
            self.far().wait_recv()

    def fan(make):
        copies = [make(i, x + d, at(x + d, y, z, lo), remote) for i, d in enumerate(steps)]
        here = c == lo

        def either(*args):
            return Either(*args, here)

        return copies + [make(3, x, partner, either)]

    def deal(g):
        def lanes(xx):
            return pl.ds(pl.multiple_of(((xx + 4) % 4) * GE + g * HD, HD), HD)

        def of_kv(i, xx, device, how):
            return how(kvsrc.at[:, :, lanes(xx)], kv.at[g, :, band + 1], kv_s.at[g, i], kv_r.at[g, band], device)

        def of_q(i, xx, device, how):
            return how(qsrc.at[:, lanes(xx)], q_in.at[g, band], q_s.at[g, i], q_r.at[g, band], device)

        return fan(of_kv) + fan(of_q)

    def dealt(g):
        copies = [remote(kvsrc.at[:, :, pl.ds(0, HD)], kv.at[g, :, b + 1], kv_s.at[g, 0], kv_r.at[g, b], partner)
                  for b in range(BANDS)]
        return copies + [remote(qsrc.at[:, pl.ds(0, HD)], q_in.at[g, b], q_s.at[g, 0], q_r.at[g, b], partner)
                         for b in range(BANDS)]

    def edges(g):
        return [
            remote(kv.at[g, :, 4], kv.at[g, :, 0], y_s.at[g, 0], y_r.at[g, 0], y_mates[0]),
            remote(kv.at[g, :, 1], kv.at[g, :, 5], y_s.at[g, 1], y_r.at[g, 1], y_mates[1]),
        ]

    def ask(g):
        return remote(q_in.at[g], q_next.at[g], n_s.at[g], n_r.at[g], earlier)

    def answer(g):
        return [
            remote(part.at[g], back.at[g], b_s.at[g], b_r.at[g], later),
            remote(stat.at[g], stat_in.at[g], st_s.at[g], st_r.at[g], later),
        ]

    def out_copies(g):
        copies = []
        for b in range(BANDS):
            xx, core = (b // 2) * 2 + c, b % 2
            copies.append(Either(
                outs.at[g, b], out_ref.at[:, pl.ds(pl.multiple_of(x * GE + g * HD, HD), HD)],
                o_s.at[g, b], o_r.at[g, x], at(xx, y, z, core), (xx == x) & (c == core),
            ))
        return copies

    flag_copies = fan(lambda i, xx, device, how: how(flags, flags_in.at[band], fx_s.at[i], fx_r.at[band], device))
    flag_next = remote(flags_in, flags_next, fz_s, fz_r, earlier)
    sink_x = [
        remote(sel.at[:, :, own_lanes(x + d)], xin.at[x], sx_s.at[i], sx_r.at[i], at(x + d, y, z, c))
        for i, d in enumerate(steps)
    ]
    sink_z = [remote(zown, zin.at[i], sz_s.at[i], sz_r.at[i], mate) for i, mate in enumerate(z_mates)]
    sink_y = [remote(skv.at[0, 0], skv.at[i + 1, 0], sy_s.at[i], sy_r.at[i], mate) for i, mate in enumerate(y_mates)]
    sink_c = [remote(skv.at[i, 0], skv.at[i, 1], sc_s.at[i], sc_r.at[i], partner) for i in range(4)]

    def start(copies):
        for copy in copies:
            copy.start()

    def landed(copies):
        for copy in copies:
            copy.wait_recv()

    def arrive(g):
        landed(dealt(g))
        start(edges(g))
        ask(g).start()
        if g + EARLY < G:
            start(deal(g + EARLY))

    def make_bias(b, carry):
        lane = lax.broadcasted_iota(jnp.int32, (1, TOK), 1)
        key_first = (lane % COLS) < TC
        query_first = (lax.broadcasted_iota(jnp.int32, (TOK, TOK), 0) % COLS) < TC
        up = jnp.where(y * BANDS + b > 0, 1.0, 0.0).astype(F32)
        down = jnp.where(y * BANDS + b < 15, 1.0, 0.0).astype(F32)
        before = jnp.where(time < 7, 1.0, 0.0).astype(F32)
        for which, (table, base) in enumerate(((flags_in, 9), (flags_next, 0))):
            mask = table[b]
            for slot in range(3):
                lines = []
                for cq in range(2):
                    pair = []
                    for ck in range(2):
                        dw = ck - cq + 1
                        code = base + slot * 3 + dw
                        value = mask[cq:cq + 1, code:code + 1]
                        if which == 0 and slot == 1 and dw == 1:
                            value = jnp.ones_like(value)
                        if slot == 0:
                            value = value * up
                        if slot == 2:
                            value = value * down
                        if which == 1:
                            value = value * before
                        pair.append(value)
                    lines.append(jnp.where(key_first, pair[0], pair[1]))
                allowed = jnp.where(query_first, lines[0], lines[1])
                bias[b, which * TOK:(which + 1) * TOK, slot * TOK:(slot + 1) * TOK] = jnp.where(
                    allowed > 0.5, 0.0, MASKED
                )
        return carry

    contract = (((1,), (1,)), ((), ()))

    def window(g):
        landed(edges(g))
        ask(g).wait_recv()
        lane = lax.broadcasted_iota(jnp.int32, (TOK, 128), 1)
        table = jnp.zeros((TOK, 128), F32)
        for b in range(BANDS):
            q = jnp.concatenate([q_in[g, b], q_next[g, b]], axis=0)
            k = kv[g, 0, b:b + 3].reshape(3 * TOK, HD)
            v = kv[g, 1, b:b + 3].reshape(3 * TOK, HD)
            scores = lax.dot_general(q, k, contract, preferred_element_type=F32) + bias[b]
            top = jnp.max(scores, axis=1, keepdims=True)
            probs = jnp.exp2((scores - top) * SCALE).astype(BF16)
            total = jnp.dot(probs, jnp.concatenate([v, ones[0:3 * TOK]], axis=1), preferred_element_type=F32)
            weighted, norm = total[:, :HD], total[:, HD:]
            ours[g, b] = weighted[:TOK]
            our_sum[g, b] = norm[:TOK]
            our_top[g, b] = jnp.broadcast_to(top[:TOK], (TOK, HD))
            part[g, b] = (weighted[TOK:] / norm[TOK:]).astype(BF16)
            table = jnp.where(lane == b, top[TOK:], jnp.where(lane == b + 4, norm[TOK:], table))
        stat[g] = table.T[0:8]
        start(answer(g))

    def finish(g):
        landed(answer(g))
        table = jnp.concatenate([stat_in[g], jnp.zeros((120, 128), F32)], axis=0).T
        lines = slice(g * HD, (g + 1) * HD)
        sink_k = skv[:, :, 0, :, lines].reshape(512, HD)
        sink_v = jnp.concatenate([skv[:, :, 1, :, lines].reshape(512, HD), ones[...]], axis=1)
        for b in range(BANDS):
            scores = lax.dot_general(q_in[g, b], sink_k, contract, preferred_element_type=F32)
            top_a, top_b, norm_b = our_top[g, b], table[:, b:b + 1], table[:, b + 4:b + 5]
            top = jnp.maximum(jnp.maximum(top_a, top_b), jnp.max(scores, axis=1, keepdims=True))
            probs = jnp.exp2((scores - top[:, 0:1]) * SCALE).astype(BF16)
            total = jnp.dot(probs, sink_v, preferred_element_type=F32)
            weight_a = jnp.exp2((top_a - top) * SCALE)
            weight_b = jnp.exp2((top_b - top) * SCALE) * norm_b
            norm = weight_a * our_sum[g, b] + weight_b + total[:, HD:]
            value = weight_a * ours[g, b] + weight_b * back[g, b].astype(F32) + total[:, :HD]
            outs[g, b] = (value / norm).astype(BF16)
        start(out_copies(g))

    start(sink_x)
    start(flag_copies)
    for g in range(EARLY):
        start(deal(g))
    xin[x] = sel[:, :, own_lanes(x)]
    for i, d in enumerate((-1, 1, 2)):
        remote(xin.at[0], xin.at[(x + d + 4) % 4], sx_s.at[i], sx_r.at[i], partner).wait_recv()
    for i in range(2):
        zown[:, i * SINK:(i + 1) * SINK] = (xin[2 * i].astype(F32) + xin[2 * i + 1].astype(F32)).astype(BF16)
    start(sink_z)
    for b in range(BANDS):
        remote(flags, flags_in.at[b], fx_s.at[0], fx_r.at[b], partner).wait_recv()
    flag_next.start()
    arrive(0)
    landed(sink_z)
    skv[0, 0] = (zown[...].astype(F32) + zin[0].astype(F32) + zin[1].astype(F32) + zin[2].astype(F32)).astype(BF16)
    start(sink_y)
    sink_c[0].start()
    flag_next.wait_recv()
    lax.fori_loop(0, BANDS, make_bias, 0)
    arrive(1)
    window(0)
    arrive(2)
    window(1)
    for i in range(3):
        sink_y[i].wait_recv()
        sink_c[i + 1].start()
    arrive(3)
    window(2)
    landed(sink_c)
    finish(0)
    arrive(4)
    window(3)
    finish(1)
    window(4)
    finish(2)
    finish(3)
    finish(4)

    for g in range(G):
        for i in range(4):
            remote(outs.at[g, 0], out_ref.at[:, pl.ds(i * GE + g * HD, HD)], o_s.at[g, 0], o_r.at[g, i], partner).wait_recv()
    sent = [*sink_x, *sink_z, *sink_y, *sink_c, *flag_copies, flag_next]
    for g in range(G):
        sent += [*deal(g), *edges(g), ask(g), *answer(g), *out_copies(g)]
    for copy in sent:
        copy.wait_send()


def shards(queries, keys, values, tile_mask, sink_frame):
    any_spec, vmem, smem = (pl.BlockSpec(memory_space=space) for space in (pl.ANY, pltpu.VMEM, pltpu.SMEM))
    sems = pltpu.SemaphoreType.DMA
    bf = lambda *shape: pltpu.VMEM(shape, BF16)
    f32 = lambda *shape: pltpu.VMEM(shape, F32)
    pairs = [
        (4,), (), (G, 4), (G, 4), (G, 2), (G,), (G,), (G,), (3,), (3,), (3,), (4,), (G, 4),
    ]
    out = pl.pallas_call(
        attend,
        out_shape=jax.ShapeDtypeStruct((TOK, E), BF16),
        in_specs=[any_spec, any_spec, any_spec, any_spec, smem],
        out_specs=vmem,
        scratch_shapes=[
            pltpu.VMEM((2, 18), jnp.int32),
            bf(TOK, E), bf(2, TOK, E),
            f32(8, 128), f32(BANDS, 8, 128), f32(BANDS, 8, 128),
            f32(BANDS, 2 * TOK, 3 * TOK),
            bf(2, SINK, E), bf(4, 2, SINK, GE), bf(2, 2 * SINK, GE), bf(3, 2, 2 * SINK, GE),
            bf(4, 2, 2, 2 * SINK, GE), bf(512, HD),
            bf(G, BANDS, TOK, HD), bf(G, BANDS, TOK, HD), bf(G, 2, BANDS + 2, TOK, HD),
            bf(G, BANDS, TOK, HD), bf(G, BANDS, TOK, HD), f32(G, 8, 128), f32(G, 8, 128),
            f32(G, BANDS, TOK, HD), f32(G, BANDS, TOK, HD), f32(G, BANDS, TOK, HD), bf(G, BANDS, TOK, HD),
            sems((4,)),
            *[sems(shape) for shape in pairs for _ in range(2)],
        ],
        compiler_params=pltpu.CompilerParams(
            collective_id=0, has_side_effects=True, vmem_limit_bytes=60 * 2**20
        ),
        cost_estimate=pl.CostEstimate(flops=2 * 10**9, bytes_accessed=3 * 10**6, transcendentals=4 * 10**6),
    )(
        queries.reshape(TOK, E), keys.reshape(TOK, E), values.reshape(TOK, E),
        tile_mask.reshape(2, 18), sink_frame,
    )
    return out.reshape(queries.shape)


def solution(mesh):
    spec = P("tm", "height", None, None)
    return jax.shard_map(
        shards,
        mesh=mesh,
        in_specs=(spec, spec, spec, spec, P()),
        out_specs=spec,
        check_vma=False,
    )
```

```python
import math

import jax
import jax.numpy as jnp
from jax import lax
from jax.experimental import pallas as pl
from jax.experimental.pallas import tpu as pltpu
from jax.sharding import PartitionSpec as P

H = 20
HD = 128
TF = 4
TC = 8
COLS = 16
E = H * HD
TOK = 128
SINK = 32
G = 5
GE = G * HD
BANDS = 4
EARLY = 2
MASKED = -1e30
SCALE = math.log2(math.e) / math.sqrt(HD)
MESH = pl.DeviceIdType.MESH
F32, BF16 = jnp.float32, jnp.bfloat16


def attend(q_hbm, k_hbm, v_hbm, mask_hbm, sink_ref, out_ref,
           mask_ref, ksrc, vsrc, flags, flags_in, flags_next, bias, sel, xin, skv, ones,
           q_in, q_next, kv, part, back, stat, stat_in, ours, our_top, our_sum, outs,
           local_sem, fx_s, fx_r, fz_s, fz_r, k_s, k_r, v_s, v_r, q_s, q_r, y_s, y_r, n_s, n_r, b_s, b_r, st_s, st_r,
           sx_s, sx_r, sy_s, sy_r, sc_s, sc_r, o_s, o_r):
    tm, h = lax.axis_index("tm"), lax.axis_index("height")
    lo, z, y, hi, c = tm // 4, tm % 4, h // 4, (h // 2) % 2, h % 2
    x = hi * 2 + lo
    time = z + 4 * c

    def at(x, y, z, c):
        x, y, z = (x + 4) % 4, (y + 4) % 4, (z + 4) % 4
        return ((x % 2) * 4 + z, y * 4 + (x // 2) * 2 + c)

    def at_time(t):
        t = (t + 8) % 8
        return at(x, y, t % 4, t // 4)

    partner = at(x, y, z, 1 - c)
    earlier, later = at_time(time - 1), at_time(time + 1)
    steps = (1, -1, 2)
    y_mates = [at(x, y + d, z, c) for d in steps]
    around = [(i, j) for i in (0, 1, -1, 2) for j in (0, 1, -1, 2) if (i, j) != (0, 0)]

    def remote(src, dst, send, recv, device):
        return pltpu.make_async_remote_copy(src, dst, send, recv, device_id=device, device_id_type=MESH)

    barrier = pltpu.get_barrier_semaphore()
    friends = [at(x + d, y, z, 1 - c) for d in steps]
    friends += [partner, earlier, later]
    friends += [at(x + dx, y, z + dz, c) for dx, dz in around]
    friends += [at(x, y + dy, z + dz, c) for dy, dz in around]
    for friend in friends:
        pl.semaphore_signal(barrier, inc=1, device_id=friend, device_id_type=MESH)
    local = [
        pltpu.make_async_copy(mask_hbm, mask_ref, local_sem.at[0]),
        pltpu.make_async_copy(k_hbm, ksrc, local_sem.at[1]),
        pltpu.make_async_copy(v_hbm, vsrc, local_sem.at[2]),
    ]
    for copy in local:
        copy.start()
    ones[...] = jnp.ones_like(ones)
    stat[...] = jnp.zeros_like(stat)
    flags[...] = jnp.zeros_like(flags)
    local[0].wait()
    flags[0:2, 0:18] = mask_ref[...].astype(F32)

    frame = (sink_ref[0] - tm * TF).astype(F32)
    for i, source in enumerate((ksrc, vsrc)):
        local[i + 1].wait()
        tokens = 0.0
        for f in range(TF):
            mine = jnp.where(frame == f, 1.0, 0.0).astype(F32)
            tokens = tokens + source[f * SINK:(f + 1) * SINK, :].astype(F32) * mine
        sel[i] = tokens.astype(BF16)
    pl.semaphore_wait(barrier, len(friends))

    def own_lanes(xx):
        return pl.ds(pl.multiple_of(((xx + 4) % 4) * GE, HD), GE)

    band = hi * 2 + c

    class Either:
        def __init__(self, src, dst, send, recv, device, here):
            self.far = lambda: remote(src, dst, send, recv, device)
            self.near = lambda: pltpu.make_async_copy(src, dst, recv)
            self.here = here

        def start(self):
            pl.when(self.here)(lambda: self.near().start())
            pl.when(jnp.logical_not(self.here))(lambda: self.far().start())

        def wait_send(self):
            pl.when(jnp.logical_not(self.here))(lambda: self.far().wait_send())

        def wait_recv(self):
            self.far().wait_recv()

    def fan(make):
        copies = [make(i, x + d, at(x + d, y, z, lo), remote) for i, d in enumerate(steps)]
        here = c == lo

        def either(*args):
            return Either(*args, here)

        return copies + [make(3, x, partner, either)]

    def deal(g):
        def lanes(xx):
            return pl.ds(pl.multiple_of(((xx + 4) % 4) * GE + g * HD, HD), HD)

        def of_k(i, xx, device, how):
            return how(k_hbm.at[:, lanes(xx)], kv.at[g, 0, band + 1], k_s.at[g, i], k_r.at[g, band], device)

        def of_v(i, xx, device, how):
            return how(v_hbm.at[:, lanes(xx)], kv.at[g, 1, band + 1], v_s.at[g, i], v_r.at[g, band], device)

        def of_q(i, xx, device, how):
            return how(q_hbm.at[:, lanes(xx)], q_in.at[g, band], q_s.at[g, i], q_r.at[g, band], device)

        return fan(of_k) + fan(of_v) + fan(of_q)

    def dealt(g):
        sample = k_hbm.at[:, pl.ds(0, HD)]
        copies = []
        for b in range(BANDS):
            copies += [
                remote(sample, kv.at[g, 0, b + 1], k_s.at[g, 0], k_r.at[g, b], partner),
                remote(sample, kv.at[g, 1, b + 1], v_s.at[g, 0], v_r.at[g, b], partner),
                remote(sample, q_in.at[g, b], q_s.at[g, 0], q_r.at[g, b], partner),
            ]
        return copies

    def edges(g):
        return [
            remote(kv.at[g, :, 4], kv.at[g, :, 0], y_s.at[g, 0], y_r.at[g, 0], y_mates[0]),
            remote(kv.at[g, :, 1], kv.at[g, :, 5], y_s.at[g, 1], y_r.at[g, 1], y_mates[1]),
        ]

    def ask(g):
        return remote(q_in.at[g], q_next.at[g], n_s.at[g], n_r.at[g], earlier)

    def answer(g, half):
        bands = pl.ds(2 * half, 2)
        return [
            remote(part.at[g, bands], back.at[g, bands], b_s.at[g, half], b_r.at[g, half], later),
            remote(stat.at[g, half], stat_in.at[g, half], st_s.at[g, half], st_r.at[g, half], later),
        ]

    def out_copies(g, half):
        copies = []
        for b in (2 * half, 2 * half + 1):
            xx, core = (b // 2) * 2 + c, b % 2
            copies.append(Either(
                outs.at[g, b], out_ref.at[:, pl.ds(pl.multiple_of(x * GE + g * HD, HD), HD)],
                o_s.at[g, b], o_r.at[g, x], at(xx, y, z, core), (xx == x) & (c == core),
            ))
        return copies

    flag_copies = fan(lambda i, xx, device, how: how(flags, flags_in.at[band], fx_s.at[i], fx_r.at[band], device))
    flag_next = remote(flags_in, flags_next, fz_s, fz_r, earlier)
    def piece_for(xx, zz):
        xx, zz = (xx + 4) % 4, (zz + 4) % 4
        rows = pl.ds(pl.multiple_of(zz % 2 * COLS, COLS), COLS)
        return sel.at[zz // 2, rows, pl.ds(pl.multiple_of(xx * GE, HD), GE)]

    def place_of(yy, zz):
        yy, zz = (yy + 4) % 4, (zz + 4) % 4
        return skv.at[yy, 0, zz // 2, zz % 2]

    sink_x = [
        remote(piece_for(x + dx, z + dz), xin.at[x, z], sx_s.at[n], sx_r.at[n], at(x + dx, y, z + dz, c))
        for n, (dx, dz) in enumerate(around)
    ]
    sink_y = [
        remote(place_of(y, z), place_of(y, z), sy_s.at[n], sy_r.at[n], at(x, y + dy, z + dz, c))
        for n, (dy, dz) in enumerate(around)
    ]

    def across(i):
        yy = (y - (0, 1, -1, 2)[i] + 4) % 4
        return remote(skv.at[yy, 0], skv.at[yy, 1], sc_s.at[i], sc_r.at[i], partner)

    def pass_on():
        for i, dy in enumerate((0, 1, -1, 2)):
            for n, offset in enumerate(around):
                if offset[0] == dy:
                    sink_y[n].wait_recv()
            across(i).start()

    def start(copies):
        for copy in copies:
            copy.start()

    def landed(copies):
        for copy in copies:
            copy.wait_recv()

    def arrive(g):
        landed(dealt(g))
        start(edges(g))
        ask(g).start()
        if g + EARLY < G:
            start(deal(g + EARLY))

    def make_bias(b, carry):
        lane = lax.broadcasted_iota(jnp.int32, (1, TOK), 1)
        key_first = (lane % COLS) < TC
        query_first = (lax.broadcasted_iota(jnp.int32, (TOK, TOK), 0) % COLS) < TC
        up = jnp.where(y * BANDS + b > 0, 1.0, 0.0).astype(F32)
        down = jnp.where(y * BANDS + b < 15, 1.0, 0.0).astype(F32)
        before = jnp.where(time < 7, 1.0, 0.0).astype(F32)
        for which, (table, base) in enumerate(((flags_in, 9), (flags_next, 0))):
            mask = table[b]
            for slot in range(3):
                lines = []
                for cq in range(2):
                    pair = []
                    for ck in range(2):
                        dw = ck - cq + 1
                        code = base + slot * 3 + dw
                        value = mask[cq:cq + 1, code:code + 1]
                        if which == 0 and slot == 1 and dw == 1:
                            value = jnp.ones_like(value)
                        if slot == 0:
                            value = value * up
                        if slot == 2:
                            value = value * down
                        if which == 1:
                            value = value * before
                        pair.append(value)
                    lines.append(jnp.where(key_first, pair[0], pair[1]))
                allowed = jnp.where(query_first, lines[0], lines[1])
                bias[b, which * TOK:(which + 1) * TOK, slot * TOK:(slot + 1) * TOK] = jnp.where(
                    allowed > 0.5, 0.0, MASKED
                )
        return carry

    contract = (((1,), (1,)), ((), ()))

    def window(g):
        landed(edges(g))
        ask(g).wait_recv()
        lane = lax.broadcasted_iota(jnp.int32, (TOK, 128), 1)
        for half in range(2):
            table = jnp.zeros((TOK, 128), F32)
            for b in (2 * half, 2 * half + 1):
                q = jnp.concatenate([q_in[g, b], q_next[g, b]], axis=0)
                k = kv[g, 0, b:b + 3].reshape(3 * TOK, HD)
                v = kv[g, 1, b:b + 3].reshape(3 * TOK, HD)
                scores = lax.dot_general(q, k, contract, preferred_element_type=F32) + bias[b]
                top = jnp.max(scores, axis=1, keepdims=True)
                probs = jnp.exp2((scores - top) * SCALE).astype(BF16)
                total = jnp.dot(probs, jnp.concatenate([v, ones[0:3 * TOK]], axis=1), preferred_element_type=F32)
                weighted, norm = total[:, :HD], total[:, HD:]
                ours[g, b] = weighted[:TOK]
                our_sum[g, b] = norm[:TOK]
                our_top[g, b] = jnp.broadcast_to(top[:TOK], (TOK, HD))
                part[g, b] = (weighted[TOK:] / norm[TOK:]).astype(BF16)
                table = jnp.where(lane == b % 2, top[TOK:], jnp.where(lane == b % 2 + 4, norm[TOK:], table))
            stat[g, half] = table.T[0:8]
            start(answer(g, half))

    def finish(g):
        lines = slice(g * HD, (g + 1) * HD)
        sink_k = skv[:, :, 0, :, :, :, lines].reshape(512, HD)
        sink_v = jnp.concatenate([skv[:, :, 1, :, :, :, lines].reshape(512, HD), ones[...]], axis=1)
        for half in range(2):
            landed(answer(g, half))
            table = jnp.concatenate([stat_in[g, half], jnp.zeros((120, 128), F32)], axis=0).T
            for b in (2 * half, 2 * half + 1):
                scores = lax.dot_general(q_in[g, b], sink_k, contract, preferred_element_type=F32)
                top_a, top_b, norm_b = our_top[g, b], table[:, b % 2:b % 2 + 1], table[:, b % 2 + 4:b % 2 + 5]
                top = jnp.maximum(jnp.maximum(top_a, top_b), jnp.max(scores, axis=1, keepdims=True))
                probs = jnp.exp2((scores - top[:, 0:1]) * SCALE).astype(BF16)
                total = jnp.dot(probs, sink_v, preferred_element_type=F32)
                weight_a = jnp.exp2((top_a - top) * SCALE)
                weight_b = jnp.exp2((top_b - top) * SCALE) * norm_b
                norm = weight_a * our_sum[g, b] + weight_b + total[:, HD:]
                value = weight_a * ours[g, b] + weight_b * back[g, b].astype(F32) + total[:, :HD]
                outs[g, b] = (value / norm).astype(BF16)
            start(out_copies(g, half))

    start(flag_copies)
    start(sink_x)
    start(deal(0))
    for g in range(1, EARLY):
        start(deal(g))
    xin[x, z] = piece_for(x, z)[...]
    landed(sink_x)
    for i in range(2):
        total = sum(xin[2 * i + j, k].astype(F32) for j in range(2) for k in range(4))
        skv[y, 0, z // 2, z % 2, i] = total.astype(BF16)
    start(sink_y)
    for b in range(BANDS):
        remote(flags, flags_in.at[b], fx_s.at[0], fx_r.at[b], partner).wait_recv()
    flag_next.start()
    arrive(0)
    flag_next.wait_recv()
    lax.fori_loop(0, BANDS, make_bias, 0)
    arrive(1)
    window(0)
    arrive(2)
    window(1)
    pass_on()
    arrive(3)
    window(2)
    landed([across(i) for i in range(4)])
    finish(0)
    arrive(4)
    window(3)
    finish(1)
    window(4)
    finish(2)
    finish(3)
    finish(4)

    for g in range(G):
        for i in range(4):
            remote(outs.at[g, 0], out_ref.at[:, pl.ds(i * GE + g * HD, HD)], o_s.at[g, 0], o_r.at[g, i], partner).wait_recv()
    sent = [*sink_x, *sink_y, *[across(i) for i in range(4)], *flag_copies, flag_next]
    for g in range(G):
        sent += [*deal(g), *edges(g), ask(g), *answer(g, 0), *answer(g, 1), *out_copies(g, 0), *out_copies(g, 1)]
    for copy in sent:
        copy.wait_send()


def shards(queries, keys, values, tile_mask, sink_frame):
    hbm, vmem, smem = (pl.BlockSpec(memory_space=space) for space in (pltpu.HBM, pltpu.VMEM, pltpu.SMEM))
    sems = pltpu.SemaphoreType.DMA
    bf = lambda *shape: pltpu.VMEM(shape, BF16)
    f32 = lambda *shape: pltpu.VMEM(shape, F32)
    pairs = [
        (4,), (), (G, 4), (G, 4), (G, 4), (G, 2), (G,), (G, 2), (G, 2), (15,), (15,), (4,), (G, 4),
    ]
    out = pl.pallas_call(
        attend,
        out_shape=jax.ShapeDtypeStruct((TOK, E), BF16),
        in_specs=[hbm, hbm, hbm, hbm, smem],
        out_specs=vmem,
        scratch_shapes=[
            pltpu.VMEM((2, 18), jnp.int32),
            bf(TOK, E), bf(TOK, E),
            f32(8, 128), f32(BANDS, 8, 128), f32(BANDS, 8, 128),
            f32(BANDS, 2 * TOK, 3 * TOK),
            bf(2, SINK, E), bf(4, 4, COLS, GE), bf(4, 2, 2, 2, 2, COLS, GE), bf(512, HD),
            bf(G, BANDS, TOK, HD), bf(G, BANDS, TOK, HD), bf(G, 2, BANDS + 2, TOK, HD),
            bf(G, BANDS, TOK, HD), bf(G, BANDS, TOK, HD), f32(G, 2, 8, 128), f32(G, 2, 8, 128),
            f32(G, BANDS, TOK, HD), f32(G, BANDS, TOK, HD), f32(G, BANDS, TOK, HD), bf(G, BANDS, TOK, HD),
            sems((4,)),
            *[sems(shape) for shape in pairs for _ in range(2)],
        ],
        compiler_params=pltpu.CompilerParams(
            collective_id=0, has_side_effects=True, vmem_limit_bytes=32 * 2**20
        ),
        cost_estimate=pl.CostEstimate(flops=2 * 10**9, bytes_accessed=3 * 10**6, transcendentals=4 * 10**6),
    )(
        *(pltpu.with_memory_space_constraint(a, pltpu.HBM) for a in (
            queries.reshape(TOK, E), keys.reshape(TOK, E), values.reshape(TOK, E), tile_mask.reshape(2, 18))),
        sink_frame,
    )
    return out.reshape(queries.shape)


def solution(mesh):
    spec = P("tm", "height", None, None)
    return jax.shard_map(
        shards,
        mesh=mesh,
        in_specs=(spec, spec, spec, spec, P()),
        out_specs=spec,
        check_vma=False,
    )
```

```python
import math

import jax
import jax.numpy as jnp
from jax import lax
from jax.experimental import pallas as pl
from jax.experimental.pallas import tpu as pltpu
from jax.sharding import PartitionSpec as P

H = 20
HD = 128
TF = 4
TC = 8
COLS = 16
E = H * HD
TOK = 128
SINK = 32
G = 5
GE = G * HD
BANDS = 4
EARLY = 2
MASKED = -1e30
SCALE = math.log2(math.e) / math.sqrt(HD)
MESH = pl.DeviceIdType.MESH
F32, BF16 = jnp.float32, jnp.bfloat16


def attend(q_hbm, k_hbm, v_hbm, mask_hbm, sink_ref, out_ref,
           mask_ref, ksrc, vsrc, flags, flags_in, flags_next, bias, sel, xin, skv, ones,
           q_in, q_next, kv, part, back, stat, stat_in, ours, our_top, our_sum, outs,
           local_sem, fx_s, fx_r, fz_s, fz_r, k_s, k_r, v_s, v_r, q_s, q_r, y_s, y_r, n_s, n_r, b_s, b_r, st_s, st_r,
           sx_s, sx_r, sy_s, sy_r, sc_s, sc_r, o_s, o_r):
    tm, h = lax.axis_index("tm"), lax.axis_index("height")
    lo, z, y, hi, c = tm // 4, tm % 4, h // 4, (h // 2) % 2, h % 2
    x = hi * 2 + lo
    time = z + 4 * c

    def at(x, y, z, c):
        x, y, z = (x + 4) % 4, (y + 4) % 4, (z + 4) % 4
        return ((x % 2) * 4 + z, y * 4 + (x // 2) * 2 + c)

    def at_time(t):
        t = (t + 8) % 8
        return at(x, y, t % 4, t // 4)

    partner = at(x, y, z, 1 - c)
    earlier, later = at_time(time - 1), at_time(time + 1)
    steps = (1, -1, 2)
    y_mates = [at(x, y + d, z, c) for d in steps]
    around = [(i, j) for i in (0, 1, -1, 2) for j in (0, 1, -1, 2) if (i, j) != (0, 0)]

    def remote(src, dst, send, recv, device):
        return pltpu.make_async_remote_copy(src, dst, send, recv, device_id=device, device_id_type=MESH)

    barrier = pltpu.get_barrier_semaphore()
    friends = [at(x + d, y, z, 1 - c) for d in steps]
    friends += [partner, earlier, later]
    friends += [at(x + dx, y, z + dz, c) for dx, dz in around]
    friends += [at(x, y + dy, z + dz, c) for dy, dz in around if dy != 0]
    for friend in friends:
        pl.semaphore_signal(barrier, inc=1, device_id=friend, device_id_type=MESH)
    local = [
        pltpu.make_async_copy(mask_hbm, mask_ref, local_sem.at[0]),
        pltpu.make_async_copy(k_hbm, ksrc, local_sem.at[1]),
        pltpu.make_async_copy(v_hbm, vsrc, local_sem.at[2]),
    ]
    for copy in local:
        copy.start()
    ones[...] = jnp.ones_like(ones)
    stat[...] = jnp.zeros_like(stat)
    flags[...] = jnp.zeros_like(flags)
    local[0].wait()
    flags[0:2, 0:18] = mask_ref[...].astype(F32)

    frame = (sink_ref[0] - tm * TF).astype(F32)
    for i, source in enumerate((ksrc, vsrc)):
        local[i + 1].wait()
        tokens = 0.0
        for f in range(TF):
            mine = jnp.where(frame == f, 1.0, 0.0).astype(F32)
            tokens = tokens + source[f * SINK:(f + 1) * SINK, :].astype(F32) * mine
        sel[i] = tokens.astype(BF16)
    pl.semaphore_wait(barrier, len(friends))

    def own_lanes(xx):
        return pl.ds(pl.multiple_of(((xx + 4) % 4) * GE, HD), GE)

    band = hi * 2 + c

    class Either:
        def __init__(self, src, dst, send, recv, device, here):
            self.far = lambda: remote(src, dst, send, recv, device)
            self.near = lambda: pltpu.make_async_copy(src, dst, recv)
            self.here = here

        def start(self):
            pl.when(self.here)(lambda: self.near().start())
            pl.when(jnp.logical_not(self.here))(lambda: self.far().start())

        def wait_send(self):
            pl.when(jnp.logical_not(self.here))(lambda: self.far().wait_send())

        def wait_recv(self):
            self.far().wait_recv()

    def fan(make):
        copies = [make(i, x + d, at(x + d, y, z, lo), remote) for i, d in enumerate(steps)]
        here = c == lo

        def either(*args):
            return Either(*args, here)

        return copies + [make(3, x, partner, either)]

    def deal(g):
        def lanes(xx):
            return pl.ds(pl.multiple_of(((xx + 4) % 4) * GE + g * HD, HD), HD)

        def of_k(i, xx, device, how):
            return how(k_hbm.at[:, lanes(xx)], kv.at[g, 0, band + 1], k_s.at[g, i], k_r.at[g, band], device)

        def of_v(i, xx, device, how):
            return how(v_hbm.at[:, lanes(xx)], kv.at[g, 1, band + 1], v_s.at[g, i], v_r.at[g, band], device)

        def of_q(i, xx, device, how):
            return how(q_hbm.at[:, lanes(xx)], q_in.at[g, band], q_s.at[g, i], q_r.at[g, band], device)

        return fan(of_k) + fan(of_v) + fan(of_q)

    def dealt(g):
        sample = k_hbm.at[:, pl.ds(0, HD)]
        copies = []
        for b in range(BANDS):
            copies += [
                remote(sample, kv.at[g, 0, b + 1], k_s.at[g, 0], k_r.at[g, b], partner),
                remote(sample, kv.at[g, 1, b + 1], v_s.at[g, 0], v_r.at[g, b], partner),
                remote(sample, q_in.at[g, b], q_s.at[g, 0], q_r.at[g, b], partner),
            ]
        return copies

    def edges(g):
        return [
            remote(kv.at[g, :, 4], kv.at[g, :, 0], y_s.at[g, 0], y_r.at[g, 0], y_mates[0]),
            remote(kv.at[g, :, 1], kv.at[g, :, 5], y_s.at[g, 1], y_r.at[g, 1], y_mates[1]),
        ]

    def ask(g):
        return remote(q_in.at[g], q_next.at[g], n_s.at[g], n_r.at[g], earlier)

    def answer(g, half):
        bands = pl.ds(2 * half, 2)
        return [
            remote(part.at[g, bands], back.at[g, bands], b_s.at[g, half], b_r.at[g, half], later),
            remote(stat.at[g, half], stat_in.at[g, half], st_s.at[g, half], st_r.at[g, half], later),
        ]

    def out_copies(g, half):
        copies = []
        for b in (2 * half, 2 * half + 1):
            xx, core = (b // 2) * 2 + c, b % 2
            copies.append(Either(
                outs.at[g, b], out_ref.at[:, pl.ds(pl.multiple_of(x * GE + g * HD, HD), HD)],
                o_s.at[g, b], o_r.at[g, x], at(xx, y, z, core), (xx == x) & (c == core),
            ))
        return copies

    flag_copies = fan(lambda i, xx, device, how: how(flags, flags_in.at[band], fx_s.at[i], fx_r.at[band], device))
    flag_next = remote(flags_in, flags_next, fz_s, fz_r, earlier)
    def piece_for(xx, zz):
        xx, zz = (xx + 4) % 4, (zz + 4) % 4
        rows = pl.ds(pl.multiple_of(zz % 2 * COLS, COLS), COLS)
        return sel.at[zz // 2, rows, pl.ds(pl.multiple_of(xx * GE, HD), GE)]

    def place_of(yy, zz):
        yy, zz = (yy + 4) % 4, (zz + 4) % 4
        return skv.at[yy, 0, zz // 2, zz % 2]

    sink_x = [
        remote(piece_for(x + dx, z + dz), xin.at[x, z], sx_s.at[n], sx_r.at[n], at(x + dx, y, z + dz, c))
        for n, (dx, dz) in enumerate(around)
    ]
    sink_y = [
        remote(place_of(y, z), place_of(y, z), sy_s.at[n], sy_r.at[n], at(x, y + dy, z + dz, c))
        for n, (dy, dz) in enumerate(around)
    ]

    def across(i):
        yy = (y - (0, 1, -1, 2)[i] + 4) % 4
        return remote(skv.at[yy, 0], skv.at[yy, 1], sc_s.at[i], sc_r.at[i], partner)

    def pass_on():
        for i, dy in enumerate((0, 1, -1, 2)):
            for n, offset in enumerate(around):
                if offset[0] == dy:
                    sink_y[n].wait_recv()
            across(i).start()

    def start(copies):
        for copy in copies:
            copy.start()

    def landed(copies):
        for copy in copies:
            copy.wait_recv()

    def arrive(g):
        landed(dealt(g))
        start(edges(g))
        ask(g).start()
        if g + EARLY < G:
            start(deal(g + EARLY))

    def make_bias(b, carry):
        lane = lax.broadcasted_iota(jnp.int32, (1, TOK), 1)
        key_first = (lane % COLS) < TC
        query_first = (lax.broadcasted_iota(jnp.int32, (TOK, TOK), 0) % COLS) < TC
        up = jnp.where(y * BANDS + b > 0, 1.0, 0.0).astype(F32)
        down = jnp.where(y * BANDS + b < 15, 1.0, 0.0).astype(F32)
        before = jnp.where(time < 7, 1.0, 0.0).astype(F32)
        for which, (table, base) in enumerate(((flags_in, 9), (flags_next, 0))):
            mask = table[b]
            for slot in range(3):
                lines = []
                for cq in range(2):
                    pair = []
                    for ck in range(2):
                        dw = ck - cq + 1
                        code = base + slot * 3 + dw
                        value = mask[cq:cq + 1, code:code + 1]
                        if which == 0 and slot == 1 and dw == 1:
                            value = jnp.ones_like(value)
                        if slot == 0:
                            value = value * up
                        if slot == 2:
                            value = value * down
                        if which == 1:
                            value = value * before
                        pair.append(value)
                    lines.append(jnp.where(key_first, pair[0], pair[1]))
                allowed = jnp.where(query_first, lines[0], lines[1])
                bias[b, which * TOK:(which + 1) * TOK, slot * TOK:(slot + 1) * TOK] = jnp.where(
                    allowed > 0.5, 0.0, MASKED
                )
        return carry

    contract = (((1,), (1,)), ((), ()))

    def window(g):
        landed(edges(g))
        ask(g).wait_recv()
        lane = lax.broadcasted_iota(jnp.int32, (TOK, 128), 1)
        for half in range(2):
            bands = (2 * half, 2 * half + 1)
            scores = [
                lax.dot_general(
                    jnp.concatenate([q_in[g, b], q_next[g, b]], axis=0), kv[g, 0, b:b + 3].reshape(3 * TOK, HD),
                    contract, preferred_element_type=F32,
                ) + bias[b]
                for b in bands
            ]
            tops = [jnp.max(score, axis=1, keepdims=True) for score in scores]
            probs = [jnp.exp2((score - top) * SCALE).astype(BF16) for score, top in zip(scores, tops)]
            totals = [
                jnp.dot(prob, jnp.concatenate([kv[g, 1, b:b + 3].reshape(3 * TOK, HD), ones[0:3 * TOK]], axis=1),
                        preferred_element_type=F32)
                for prob, b in zip(probs, bands)
            ]
            table = jnp.zeros((TOK, 128), F32)
            for i, (b, top, total) in enumerate(zip(bands, tops, totals)):
                part[g, b] = (total[TOK:, :HD] / total[TOK:, HD:]).astype(BF16)
                table = jnp.where(lane == i, top[TOK:], jnp.where(lane == i + 4, total[TOK:, HD:], table))
            stat[g, half] = table.T[0:8]
            start(answer(g, half))
            for b, top, total in zip(bands, tops, totals):
                ours[g, b] = total[:TOK, :HD]
                our_sum[g, b] = total[:TOK, HD:]
                our_top[g, b] = jnp.broadcast_to(top[:TOK], (TOK, HD))

    def finish(g):
        lines = slice(g * HD, (g + 1) * HD)
        sink_k = skv[:, :, 0, :, :, :, lines].reshape(512, HD)
        sink_v = jnp.concatenate([skv[:, :, 1, :, :, :, lines].reshape(512, HD), ones[...]], axis=1)
        for half in range(2):
            landed(answer(g, half))
            table = jnp.concatenate([stat_in[g, half], jnp.zeros((120, 128), F32)], axis=0).T
            bands = pl.ds(2 * half, 2)
            scores = lax.dot_general(
                q_in[g, bands].reshape(2 * TOK, HD), sink_k, contract, preferred_element_type=F32
            )
            top_a, top_b, norm_b = (
                our_top[g, bands].reshape(2 * TOK, HD),
                *(jnp.concatenate([table[:, i:i + 1], table[:, i + 1:i + 2]], axis=0) for i in (0, 4)),
            )
            top = jnp.maximum(jnp.maximum(top_a, top_b), jnp.max(scores, axis=1, keepdims=True))
            probs = jnp.exp2((scores - top[:, 0:1]) * SCALE).astype(BF16)
            total = jnp.dot(probs, sink_v, preferred_element_type=F32)
            weight_a = jnp.exp2((top_a - top) * SCALE)
            weight_b = jnp.exp2((top_b - top) * SCALE) * norm_b
            norm = weight_a * our_sum[g, bands].reshape(2 * TOK, HD) + weight_b + total[:, HD:]
            value = (
                weight_a * ours[g, bands].reshape(2 * TOK, HD)
                + weight_b * back[g, bands].reshape(2 * TOK, HD).astype(F32) + total[:, :HD]
            )
            outs[g, bands] = (value / norm).astype(BF16).reshape(2, TOK, HD)
            start(out_copies(g, half))

    start(flag_copies)
    start(sink_x)
    start(deal(0))
    for g in range(1, EARLY):
        start(deal(g))
    xin[x, z] = piece_for(x, z)[...]
    landed(sink_x)
    for i in range(2):
        total = sum(xin[2 * i + j, k].astype(F32) for j in range(2) for k in range(4))
        skv[y, 0, z // 2, z % 2, i] = total.astype(BF16)
    start(sink_y)
    for b in range(BANDS):
        remote(flags, flags_in.at[b], fx_s.at[0], fx_r.at[b], partner).wait_recv()
    flag_next.start()
    arrive(0)
    flag_next.wait_recv()
    lax.fori_loop(0, BANDS, make_bias, 0)
    arrive(1)
    window(0)
    arrive(2)
    window(1)
    pass_on()
    arrive(3)
    window(2)
    arrive(4)
    landed([across(i) for i in range(4)])
    finish(0)
    window(3)
    finish(1)
    window(4)
    finish(2)
    sent = [*sink_x, *sink_y, *[across(i) for i in range(4)], *flag_copies, flag_next]
    for g in range(G):
        sent += [*deal(g), *edges(g), ask(g)]
    for g in range(2):
        sent += [*answer(g, 0), *answer(g, 1), *out_copies(g, 0), *out_copies(g, 1)]
    for copy in sent:
        copy.wait_send()
    finish(3)
    finish(4)

    for g in range(G):
        for i in range(4):
            remote(outs.at[g, 0], out_ref.at[:, pl.ds(i * GE + g * HD, HD)], o_s.at[g, 0], o_r.at[g, i], partner).wait_recv()
    for g in range(2, G):
        sent = [*answer(g, 0), *answer(g, 1), *out_copies(g, 0), *out_copies(g, 1)]
        for copy in sent:
            copy.wait_send()


def shards(queries, keys, values, tile_mask, sink_frame):
    hbm, vmem, smem = (pl.BlockSpec(memory_space=space) for space in (pltpu.HBM, pltpu.VMEM, pltpu.SMEM))
    sems = pltpu.SemaphoreType.DMA
    bf = lambda *shape: pltpu.VMEM(shape, BF16)
    f32 = lambda *shape: pltpu.VMEM(shape, F32)
    pairs = [
        (4,), (), (G, 4), (G, 4), (G, 4), (G, 2), (G,), (G, 2), (G, 2), (15,), (15,), (4,), (G, 4),
    ]
    out = pl.pallas_call(
        attend,
        out_shape=jax.ShapeDtypeStruct((TOK, E), BF16),
        in_specs=[hbm, hbm, hbm, hbm, smem],
        out_specs=vmem,
        scratch_shapes=[
            pltpu.VMEM((2, 18), jnp.int32),
            bf(TOK, E), bf(TOK, E),
            f32(8, 128), f32(BANDS, 8, 128), f32(BANDS, 8, 128),
            f32(BANDS, 2 * TOK, 3 * TOK),
            bf(2, SINK, E), bf(4, 4, COLS, GE), bf(4, 2, 2, 2, 2, COLS, GE), bf(512, HD),
            bf(G, BANDS, TOK, HD), bf(G, BANDS, TOK, HD), bf(G, 2, BANDS + 2, TOK, HD),
            bf(G, BANDS, TOK, HD), bf(G, BANDS, TOK, HD), f32(G, 2, 8, 128), f32(G, 2, 8, 128),
            f32(G, BANDS, TOK, HD), f32(G, BANDS, TOK, HD), f32(G, BANDS, TOK, HD), bf(G, BANDS, TOK, HD),
            sems((4,)),
            *[sems(shape) for shape in pairs for _ in range(2)],
        ],
        compiler_params=pltpu.CompilerParams(
            collective_id=0, has_side_effects=True, vmem_limit_bytes=32 * 2**20
        ),
        cost_estimate=pl.CostEstimate(flops=2 * 10**9, bytes_accessed=3 * 10**6, transcendentals=4 * 10**6),
    )(
        *(pltpu.with_memory_space_constraint(a, pltpu.HBM) for a in (
            queries.reshape(TOK, E), keys.reshape(TOK, E), values.reshape(TOK, E), tile_mask.reshape(2, 18))),
        sink_frame,
    )
    return out.reshape(queries.shape)


def solution(mesh):
    spec = P("tm", "height", None, None)
    return jax.shard_map(
        shards,
        mesh=mesh,
        in_specs=(spec, spec, spec, spec, P()),
        out_specs=spec,
        check_vma=False,
    )
```

```python
import math

import jax
import jax.numpy as jnp
from jax import lax
from jax.experimental import pallas as pl
from jax.experimental.pallas import tpu as pltpu
from jax.sharding import PartitionSpec as P

H = 20
HD = 128
TF = 4
TC = 8
COLS = 16
E = H * HD
TOK = 128
SINK = 32
G = 5
GE = G * HD
BANDS = 4
EARLY = 2
MASKED = -1e30
SCALE = math.log2(math.e) / math.sqrt(HD)
MESH = pl.DeviceIdType.MESH
F32, BF16 = jnp.float32, jnp.bfloat16


def attend(q_hbm, k_hbm, v_hbm, mask_hbm, sink_ref, out_ref,
           mask_ref, ksrc, vsrc, flags, flags_in, flags_next, bias, sel, xin, skv, ones,
           q_in, q_next, kv, part, back, stat, stat_in, ours, our_top, our_sum, outs,
           local_sem, fx_s, fx_r, fz_s, fz_r, k_s, k_r, v_s, v_r, q_s, q_r, y_s, y_r, n_s, n_r, b_s, b_r, st_s, st_r,
           sx_s, sx_r, sy_s, sy_r, sc_s, sc_r, o_s, o_r):
    tm, h = lax.axis_index("tm"), lax.axis_index("height")
    lo, z, y, hi, c = tm // 4, tm % 4, h // 4, (h // 2) % 2, h % 2
    x = hi * 2 + lo
    time = z + 4 * c

    def at(x, y, z, c):
        x, y, z = (x + 4) % 4, (y + 4) % 4, (z + 4) % 4
        return ((x % 2) * 4 + z, y * 4 + (x // 2) * 2 + c)

    def at_time(t):
        t = (t + 8) % 8
        return at(x, y, t % 4, t // 4)

    partner = at(x, y, z, 1 - c)
    earlier, later = at_time(time - 1), at_time(time + 1)
    steps = (1, -1, 2)
    y_mates = [at(x, y + d, z, c) for d in steps]
    around = [(i, j) for i in (0, 1, -1, 2) for j in (0, 1, -1, 2) if (i, j) != (0, 0)]

    def remote(src, dst, send, recv, device):
        return pltpu.make_async_remote_copy(src, dst, send, recv, device_id=device, device_id_type=MESH)

    barrier = pltpu.get_barrier_semaphore()
    friends = [at(x + d, y, z, 1 - c) for d in steps]
    friends += [partner, earlier, later]
    friends += [at(x + dx, y, z + dz, c) for dx, dz in around]
    friends += [at(x, y + dy, z + dz, c) for dy, dz in around if dy != 0]
    for friend in friends:
        pl.semaphore_signal(barrier, inc=1, device_id=friend, device_id_type=MESH)
    local = [
        pltpu.make_async_copy(mask_hbm, mask_ref, local_sem.at[0]),
        pltpu.make_async_copy(k_hbm, ksrc, local_sem.at[1]),
        pltpu.make_async_copy(v_hbm, vsrc, local_sem.at[2]),
    ]
    for copy in local:
        copy.start()
    ones[...] = jnp.ones_like(ones)
    stat[...] = jnp.zeros_like(stat)
    flags[...] = jnp.zeros_like(flags)
    local[0].wait()
    flags[0:2, 0:18] = mask_ref[...].astype(F32)

    frame = (sink_ref[0] - tm * TF).astype(F32)
    for i, source in enumerate((ksrc, vsrc)):
        local[i + 1].wait()
        tokens = 0.0
        for f in range(TF):
            mine = jnp.where(frame == f, 1.0, 0.0).astype(F32)
            tokens = tokens + source[f * SINK:(f + 1) * SINK, :].astype(F32) * mine
        sel[i] = tokens.astype(BF16)
    pl.semaphore_wait(barrier, len(friends))

    def own_lanes(xx):
        return pl.ds(pl.multiple_of(((xx + 4) % 4) * GE, HD), GE)

    band = hi * 2 + c

    class Either:
        def __init__(self, src, dst, send, recv, device, here):
            self.far = lambda: remote(src, dst, send, recv, device)
            self.near = lambda: pltpu.make_async_copy(src, dst, recv)
            self.here = here

        def start(self):
            pl.when(self.here)(lambda: self.near().start())
            pl.when(jnp.logical_not(self.here))(lambda: self.far().start())

        def wait_send(self):
            pl.when(jnp.logical_not(self.here))(lambda: self.far().wait_send())

        def wait_recv(self):
            self.far().wait_recv()

    def fan(make):
        copies = [make(i, x + d, at(x + d, y, z, lo), remote) for i, d in ((2, 2), (0, 1), (1, -1))]
        here = c == lo

        def either(*args):
            return Either(*args, here)

        return copies + [make(3, x, partner, either)]

    def deal(g):
        def lanes(xx):
            return pl.ds(pl.multiple_of(((xx + 4) % 4) * GE + g * HD, HD), HD)

        def of_k(i, xx, device, how):
            return how(k_hbm.at[:, lanes(xx)], kv.at[g, 0, band + 1], k_s.at[g, i], k_r.at[g, band], device)

        def of_v(i, xx, device, how):
            return how(v_hbm.at[:, lanes(xx)], kv.at[g, 1, band + 1], v_s.at[g, i], v_r.at[g, band], device)

        def of_q(i, xx, device, how):
            return how(q_hbm.at[:, lanes(xx)], q_in.at[g, band], q_s.at[g, i], q_r.at[g, band], device)

        return fan(of_k) + fan(of_v) + fan(of_q)

    def dealt(g):
        sample = k_hbm.at[:, pl.ds(0, HD)]
        copies = []
        for b in range(BANDS):
            copies += [
                remote(sample, kv.at[g, 0, b + 1], k_s.at[g, 0], k_r.at[g, b], partner),
                remote(sample, kv.at[g, 1, b + 1], v_s.at[g, 0], v_r.at[g, b], partner),
                remote(sample, q_in.at[g, b], q_s.at[g, 0], q_r.at[g, b], partner),
            ]
        return copies

    def edges(g):
        return [
            remote(kv.at[g, :, 4], kv.at[g, :, 0], y_s.at[g, 0], y_r.at[g, 0], y_mates[0]),
            remote(kv.at[g, :, 1], kv.at[g, :, 5], y_s.at[g, 1], y_r.at[g, 1], y_mates[1]),
        ]

    def ask(g):
        return remote(q_in.at[g], q_next.at[g], n_s.at[g], n_r.at[g], earlier)

    def answer(g, half):
        bands = pl.ds(2 * half, 2)
        return [
            remote(part.at[g, bands], back.at[g, bands], b_s.at[g, half], b_r.at[g, half], later),
            remote(stat.at[g, half], stat_in.at[g, half], st_s.at[g, half], st_r.at[g, half], later),
        ]

    def out_copies(g, half):
        copies = []
        for b in (2 * half, 2 * half + 1):
            xx, core = (b // 2) * 2 + c, b % 2
            copies.append(Either(
                outs.at[g, b], out_ref.at[:, pl.ds(pl.multiple_of(x * GE + g * HD, HD), HD)],
                o_s.at[g, b], o_r.at[g, x], at(xx, y, z, core), (xx == x) & (c == core),
            ))
        return copies

    flag_copies = fan(lambda i, xx, device, how: how(flags, flags_in.at[band], fx_s.at[i], fx_r.at[band], device))
    flag_next = remote(flags_in, flags_next, fz_s, fz_r, earlier)
    def piece_for(xx, zz):
        xx, zz = (xx + 4) % 4, (zz + 4) % 4
        rows = pl.ds(pl.multiple_of(zz % 2 * COLS, COLS), COLS)
        return sel.at[zz // 2, rows, pl.ds(pl.multiple_of(xx * GE, HD), GE)]

    def place_of(yy, zz):
        yy, zz = (yy + 4) % 4, (zz + 4) % 4
        return skv.at[yy, 0, zz // 2, zz % 2]

    sink_x = [
        remote(piece_for(x + dx, z + dz), xin.at[x, z], sx_s.at[n], sx_r.at[n], at(x + dx, y, z + dz, c))
        for n, (dx, dz) in enumerate(around)
    ]
    sink_y = [
        remote(place_of(y, z), place_of(y, z), sy_s.at[n], sy_r.at[n], at(x, y + dy, z + dz, c))
        for n, (dy, dz) in enumerate(around)
    ]

    def across(i):
        yy = (y - (0, 1, -1, 2)[i] + 4) % 4
        return remote(skv.at[yy, 0], skv.at[yy, 1], sc_s.at[i], sc_r.at[i], partner)

    def pass_on():
        for i, dy in enumerate((0, 1, -1, 2)):
            for n, offset in enumerate(around):
                if offset[0] == dy:
                    sink_y[n].wait_recv()
            across(i).start()

    def start(copies):
        for copy in copies:
            copy.start()

    def landed(copies):
        for copy in copies:
            copy.wait_recv()

    def arrive(g):
        landed(dealt(g))
        start(edges(g))
        ask(g).start()
        if g + EARLY < G:
            start(deal(g + EARLY))

    def make_bias(b, carry):
        lane = lax.broadcasted_iota(jnp.int32, (1, TOK), 1)
        key_first = (lane % COLS) < TC
        query_first = (lax.broadcasted_iota(jnp.int32, (TOK, TOK), 0) % COLS) < TC
        up = jnp.where(y * BANDS + b > 0, 1.0, 0.0).astype(F32)
        down = jnp.where(y * BANDS + b < 15, 1.0, 0.0).astype(F32)
        before = jnp.where(time < 7, 1.0, 0.0).astype(F32)
        for which, (table, base) in enumerate(((flags_in, 9), (flags_next, 0))):
            mask = table[b]
            for slot in range(3):
                lines = []
                for cq in range(2):
                    pair = []
                    for ck in range(2):
                        dw = ck - cq + 1
                        code = base + slot * 3 + dw
                        value = mask[cq:cq + 1, code:code + 1]
                        if which == 0 and slot == 1 and dw == 1:
                            value = jnp.ones_like(value)
                        if slot == 0:
                            value = value * up
                        if slot == 2:
                            value = value * down
                        if which == 1:
                            value = value * before
                        pair.append(value)
                    lines.append(jnp.where(key_first, pair[0], pair[1]))
                allowed = jnp.where(query_first, lines[0], lines[1])
                bias[b, which * TOK:(which + 1) * TOK, slot * TOK:(slot + 1) * TOK] = jnp.where(
                    allowed > 0.5, 0.0, MASKED
                )
        return carry

    contract = (((1,), (1,)), ((), ()))

    def window(g):
        landed(edges(g))
        ask(g).wait_recv()
        lane = lax.broadcasted_iota(jnp.int32, (TOK, 128), 1)
        for half in range(2):
            bands = (2 * half, 2 * half + 1)
            scores = [
                lax.dot_general(
                    jnp.concatenate([q_in[g, b], q_next[g, b]], axis=0), kv[g, 0, b:b + 3].reshape(3 * TOK, HD),
                    contract, preferred_element_type=F32,
                ) + bias[b]
                for b in bands
            ]
            tops = [jnp.max(score, axis=1, keepdims=True) for score in scores]
            probs = [jnp.exp2((score - top) * SCALE).astype(BF16) for score, top in zip(scores, tops)]
            totals = [
                jnp.dot(prob, jnp.concatenate([kv[g, 1, b:b + 3].reshape(3 * TOK, HD), ones[0:3 * TOK]], axis=1),
                        preferred_element_type=F32)
                for prob, b in zip(probs, bands)
            ]
            table = jnp.zeros((TOK, 128), F32)
            for i, (b, top, total) in enumerate(zip(bands, tops, totals)):
                part[g, b] = (total[TOK:, :HD] / total[TOK:, HD:]).astype(BF16)
                table = jnp.where(lane == i, top[TOK:], jnp.where(lane == i + 4, total[TOK:, HD:], table))
            stat[g, half] = table.T[0:8]
            start(answer(g, half))
            for b, top, total in zip(bands, tops, totals):
                ours[g, b] = total[:TOK, :HD]
                our_sum[g, b] = total[:TOK, HD:]
                our_top[g, b] = jnp.broadcast_to(top[:TOK], (TOK, HD))

    def finish(g):
        lines = slice(g * HD, (g + 1) * HD)
        sink_k = skv[:, :, 0, :, :, :, lines].reshape(512, HD)
        sink_v = jnp.concatenate([skv[:, :, 1, :, :, :, lines].reshape(512, HD), ones[...]], axis=1)
        for half in range(2):
            landed(answer(g, half))
            table = jnp.concatenate([stat_in[g, half], jnp.zeros((120, 128), F32)], axis=0).T
            bands = pl.ds(2 * half, 2)
            scores = lax.dot_general(
                q_in[g, bands].reshape(2 * TOK, HD), sink_k, contract, preferred_element_type=F32
            )
            top_a, top_b, norm_b = (
                our_top[g, bands].reshape(2 * TOK, HD),
                *(jnp.concatenate([table[:, i:i + 1], table[:, i + 1:i + 2]], axis=0) for i in (0, 4)),
            )
            top = jnp.maximum(jnp.maximum(top_a, top_b), jnp.max(scores, axis=1, keepdims=True))
            probs = jnp.exp2((scores - top[:, 0:1]) * SCALE).astype(BF16)
            total = jnp.dot(probs, sink_v, preferred_element_type=F32)
            weight_a = jnp.exp2((top_a - top) * SCALE)
            weight_b = jnp.exp2((top_b - top) * SCALE) * norm_b
            norm = weight_a * our_sum[g, bands].reshape(2 * TOK, HD) + weight_b + total[:, HD:]
            value = (
                weight_a * ours[g, bands].reshape(2 * TOK, HD)
                + weight_b * back[g, bands].reshape(2 * TOK, HD).astype(F32) + total[:, :HD]
            )
            outs[g, bands] = (value / norm).astype(BF16).reshape(2, TOK, HD)
            start(out_copies(g, half))

    start(flag_copies)
    start(sink_x)
    start(deal(0))
    for g in range(1, EARLY):
        start(deal(g))
    xin[x, z] = piece_for(x, z)[...]
    landed(sink_x)
    for i in range(2):
        total = sum(xin[2 * i + j, k].astype(F32) for j in range(2) for k in range(4))
        skv[y, 0, z // 2, z % 2, i] = total.astype(BF16)
    start(sink_y)
    for b in range(BANDS):
        remote(flags, flags_in.at[b], fx_s.at[0], fx_r.at[b], partner).wait_recv()
    flag_next.start()
    arrive(0)
    flag_next.wait_recv()
    lax.fori_loop(0, BANDS, make_bias, 0)
    arrive(1)
    window(0)
    arrive(2)
    window(1)
    pass_on()
    arrive(3)
    window(2)
    arrive(4)
    landed([across(i) for i in range(4)])
    finish(0)
    window(3)
    finish(1)
    window(4)
    finish(2)
    sent = [*sink_x, *sink_y, *[across(i) for i in range(4)], *flag_copies, flag_next]
    for g in range(G):
        sent += [*deal(g), *edges(g), ask(g)]
    for g in range(2):
        sent += [*answer(g, 0), *answer(g, 1), *out_copies(g, 0), *out_copies(g, 1)]
    for copy in sent:
        copy.wait_send()
    finish(3)
    finish(4)

    for g in range(G):
        for i in range(4):
            remote(outs.at[g, 0], out_ref.at[:, pl.ds(i * GE + g * HD, HD)], o_s.at[g, 0], o_r.at[g, i], partner).wait_recv()
    for g in range(2, G):
        sent = [*answer(g, 0), *answer(g, 1), *out_copies(g, 0), *out_copies(g, 1)]
        for copy in sent:
            copy.wait_send()


def shards(queries, keys, values, tile_mask, sink_frame):
    hbm, vmem, smem = (pl.BlockSpec(memory_space=space) for space in (pltpu.HBM, pltpu.VMEM, pltpu.SMEM))
    sems = pltpu.SemaphoreType.DMA
    bf = lambda *shape: pltpu.VMEM(shape, BF16)
    f32 = lambda *shape: pltpu.VMEM(shape, F32)
    pairs = [
        (4,), (), (G, 4), (G, 4), (G, 4), (G, 2), (G,), (G, 2), (G, 2), (15,), (15,), (4,), (G, 4),
    ]
    out = pl.pallas_call(
        attend,
        out_shape=jax.ShapeDtypeStruct((TOK, E), BF16),
        in_specs=[hbm, hbm, hbm, hbm, smem],
        out_specs=vmem,
        scratch_shapes=[
            pltpu.VMEM((2, 18), jnp.int32),
            bf(TOK, E), bf(TOK, E),
            f32(8, 128), f32(BANDS, 8, 128), f32(BANDS, 8, 128),
            f32(BANDS, 2 * TOK, 3 * TOK),
            bf(2, SINK, E), bf(4, 4, COLS, GE), bf(4, 2, 2, 2, 2, COLS, GE), bf(512, HD),
            bf(G, BANDS, TOK, HD), bf(G, BANDS, TOK, HD), bf(G, 2, BANDS + 2, TOK, HD),
            bf(G, BANDS, TOK, HD), bf(G, BANDS, TOK, HD), f32(G, 2, 8, 128), f32(G, 2, 8, 128),
            f32(G, BANDS, TOK, HD), f32(G, BANDS, TOK, HD), f32(G, BANDS, TOK, HD), bf(G, BANDS, TOK, HD),
            sems((4,)),
            *[sems(shape) for shape in pairs for _ in range(2)],
        ],
        compiler_params=pltpu.CompilerParams(
            collective_id=0, has_side_effects=True, vmem_limit_bytes=32 * 2**20
        ),
        cost_estimate=pl.CostEstimate(flops=2 * 10**9, bytes_accessed=3 * 10**6, transcendentals=4 * 10**6),
    )(
        *(pltpu.with_memory_space_constraint(a, pltpu.HBM) for a in (
            queries.reshape(TOK, E), keys.reshape(TOK, E), values.reshape(TOK, E), tile_mask.reshape(2, 18))),
        sink_frame,
    )
    return out.reshape(queries.shape)


def solution(mesh):
    spec = P("tm", "height", None, None)
    return jax.shard_map(
        shards,
        mesh=mesh,
        in_specs=(spec, spec, spec, spec, P()),
        out_specs=spec,
        check_vma=False,
    )
```
